128 devices in a mesh: text: 4 (over z_lo, core), img: 32 (over z_hi, x, y).
Axes of the slice: x: 4, y: 4, z: 4 (z_hi: 2, z_lo: 2; z = z_hi * 2 + z_lo), core: 2. Of those that a mesh axis runs over, the one named last changes fastest.
Arguments:
- text_in: bfloat16 [8192, 8192], P('img'), may hold values from -6 to 6
- w_query: bfloat16 [8192, 4096], P(None, 'text'), may hold values from -0.0625 to 0.0625
- gate: float32 [4096], P('text'), may hold values from -1.5 to 1.5
- image_keys: bfloat16 [2048, 4096], P('img', 'text'), may hold values from -320 to 320
- image_values: bfloat16 [2048, 4096], P('img', 'text'), may hold values from -6 to 6
- image_owner: int32 [2048], P('img'), may hold values from 0 to 7, as said below
- text_image: int32 [8192], P('img'), may hold values from 0 to 7
- cotangent: bfloat16 [8192, 4096], P('img', 'text'), may hold values from -6 to 6
Outputs:
- attended: bfloat16 [8192, 4096], P('img', 'text')
- input_grad: bfloat16 [8192, 8192], P('img', 'text')
- query_weight_grad: float32 [8192, 4096], P('img', 'text')
- gate_grad: float32 [4096], P('text')
The draws below stay inside these ranges and needn't reach their ends.
Inputs may be any that keep to these rules, and one draw needn't show every extreme that they name: `image_owner`: image tokens of one image form one contiguous run in increasing image order; every image has a token; the largest image has exactly 512 tokens.
All inputs are finite; a program needn't handle non-finite values.
Results may differ from the reference program's by a relative error of at most 0.03.
The reference program's roundings to bfloat16 on the way count: a program that leaves them out, or rounds other values in their place, can miss the bound.
Values may be sent and summed in bfloat16 or wider, within the bound.
No kernel may reach another device: no remote copies, remote signals or barrier semaphores. Data moves between devices by JAX's collectives and lax.ppermute only.
A program may use at most 128 MiB of HBM per device.

```python
import math
import jax
import jax.numpy as jnp
import numpy as np
from jax import lax

D = 8192
HEADS = 32
HEAD_DIM = 128
TOK_DEV = 256
IMAGES = 8
CH = 4096
TEXT = 8192
IMG = 2048
N_IMG = 32


def owner_layout(key):
    key = jax.random.fold_in(key, 29)
    pick_key, weight_key = jax.random.split(key)
    largest = jax.random.randint(pick_key, (), 0, IMAGES)
    shares = jax.random.randint(weight_key, (IMAGES,), 2, 5).astype(jnp.int32)
    index = jnp.arange(IMAGES, dtype=jnp.int32)
    others = (index != largest).astype(jnp.int32)
    biggest = IMG // 4
    spare = IMG - biggest - (IMAGES - 1)
    shares = shares * others
    extra = (spare * shares // jnp.sum(shares)).astype(jnp.int32)
    leftover = spare - jnp.sum(extra)
    rank_among = (jnp.cumsum(others) - others).astype(jnp.int32)
    extra = extra + others * (rank_among < leftover).astype(jnp.int32)
    lengths = jnp.where(others == 1, 1 + extra, biggest).astype(jnp.int32)
    ends = jnp.cumsum(lengths).astype(jnp.int32)
    starts = ends - lengths
    position = jnp.arange(IMG, dtype=jnp.int32)
    owner = jnp.sum((position[:, None] >= ends[None, :IMAGES - 1]).astype(jnp.int32), axis=1).astype(jnp.int32)
    start_of = jnp.sum(jnp.where(owner[:, None] == index[None, :], starts[None, :], 0), axis=1).astype(jnp.int32)
    return (owner, position - start_of)


def draw_image_owner(key, part):
    owner, inside = owner_layout(key)
    return owner.astype(jnp.int32)


def draw_image_keys(key, part):
    owner, inside = owner_layout(key)
    key = jax.random.fold_in(key, 11)
    first, second = jax.random.split(key)
    base = jnp.clip(jax.random.normal(first, (IMG, CH), jnp.float32), -8.0, 8.0)
    leading = (inside < 2)[:, None]
    small = jnp.exp(jax.random.uniform(second, (IMG, 1), jnp.float32, math.log(0.5), math.log(1.5)))
    spread = jnp.where(leading, 16.0, small)
    return (base * spread).astype(jnp.bfloat16)


def with_ends(entries, stream_key, low, top_value):
    dims = entries.shape
    index_at = [jax.random.randint(jax.random.fold_in(stream_key, axis), (), 0, dims[axis]) for axis in range(len(dims))]
    entries = entries.at[tuple(index_at)].set(low)
    longest = dims.index(max(dims))
    index_at[longest] = (index_at[longest] + 1) % dims[longest]
    return entries.at[tuple(index_at)].set(top_value)


def shard_levels(stream_key, extent, cuts, least, top_value):
    loudness, own = 1.0, jax.random.fold_in(stream_key, 6)
    for dim, parts in cuts:
        heights = jnp.exp(jax.random.uniform(jax.random.fold_in(own, dim), (parts,), jnp.float32, least / len(cuts), top_value / len(cuts)))
        loudness = loudness * jnp.repeat(heights, extent[dim] // parts).reshape([-1 if axis == dim else 1 for axis in range(len(extent))])
    return loudness


def rank_bounds(amount, skew):
    portions = [(1 << 20) // math.isqrt(rank ** skew) + 1 for rank in range(1, amount + 1)]
    scale = 1 + sum(portions) // (1 << 30)
    return np.cumsum(np.array([max(1, weight // scale) for weight in portions]))


def ranked(key, extent, amount, skew):
    table = rank_bounds(amount, skew)
    pick = jax.random.randint(jax.random.fold_in(key, 1), extent, 0, int(table[amount - 1]))
    rank = jnp.searchsorted(jnp.asarray(table, jnp.int32), pick, side="right")
    return jax.random.permutation(jax.random.fold_in(key, 2), amount)[rank].astype(jnp.int32)


def gaussian(rng, shape, scale, bound, shards=(), kind=jnp.bfloat16):
    values = scale * jax.random.normal(rng, shape, jnp.float32)
    if shards:
        values = values * shard_levels(rng, shape, shards, -0.22, 0.18)
    return jnp.clip(values, -bound, bound).astype(kind)


def setup_inputs(seed: int = 0) -> dict:
    streams_of = jax.random.split(jax.random.key(seed), 9)
    text_in = gaussian(streams_of[0], (TEXT, D), 1.0, 6.0, ((0, 32),))
    w_query = gaussian(streams_of[1], (D, CH), D ** -0.5, 0.0625, ((1, 4),))
    gate = jnp.clip(jax.random.uniform(streams_of[2], (CH,), jnp.float32, -1.5, 1.5) * shard_levels(streams_of[2], (CH,), ((0, 4),), -0.4, 0.0), -1.5, 1.5)
    image_keys = draw_image_keys(jax.random.fold_in(streams_of[8], 71), 0)
    image_values = gaussian(streams_of[4], (IMG, CH), 1.0, 6.0, ((0, 32), (1, 4)))
    image_owner = draw_image_owner(jax.random.fold_in(streams_of[8], 71), 0)
    text_image = with_ends(ranked(streams_of[6], (TEXT,), IMAGES, 2), jax.random.fold_in(streams_of[6], 3), 0, IMAGES - 1).astype(jnp.int32)
    cotangent = gaussian(streams_of[7], (TEXT, CH), 1.0, 6.0, ((0, 32), (1, 4)))
    return {"text_in": text_in, "w_query": w_query, "gate": gate, "image_keys": image_keys, "image_values": image_values, "image_owner": image_owner, "text_image": text_image, "cotangent": cotangent}


EPS = 1e-06
NEG = -1e+30

def reference(text_in, w_query, gate, image_keys, image_values, image_owner, text_image, cotangent):
    text_float = text_in.astype(jnp.float32)
    inverse_rms = lax.rsqrt(lax.optimization_barrier(jnp.mean(text_float * text_float, axis=1, keepdims=True)) + EPS)
    normed = text_float * inverse_rms
    normed_bf = normed.astype(jnp.bfloat16)
    query = jnp.dot(normed_bf, w_query, preferred_element_type=jnp.float32).astype(jnp.bfloat16)
    allowed = image_owner[None, :] == text_image[:, None]
    gate_tanh = jnp.tanh(gate)
    upstream = cotangent.astype(jnp.float32)
    scale = 1.0 / math.sqrt(HEAD_DIM)

    def split_heads(array, count):
        return array.reshape(count, HEADS, HEAD_DIM).transpose(1, 0, 2)

    def one_head(inputs):
        query_head, keys_head, values_head, upstream_head, tanh_head = inputs
        scores = jnp.dot(query_head, keys_head.T, preferred_element_type=jnp.float32) * scale
        scores = jnp.where(allowed, scores, NEG)
        peak = lax.optimization_barrier(jnp.max(scores, axis=1, keepdims=True))
        weights = jnp.where(allowed, jnp.exp(scores - peak), 0.0)
        total = lax.optimization_barrier(jnp.sum(weights, axis=1, keepdims=True))
        attn = jnp.dot(weights.astype(jnp.bfloat16), values_head, preferred_element_type=jnp.float32) / total
        out_grad = upstream_head * tanh_head[None, :]
        delta = lax.optimization_barrier(jnp.sum(out_grad * attn, axis=1, keepdims=True))
        dprob = jnp.dot(out_grad.astype(jnp.bfloat16), values_head.T, preferred_element_type=jnp.float32)
        dscore = (weights / total * (dprob - delta)).astype(jnp.bfloat16)
        grad = (jnp.dot(dscore, keys_head, preferred_element_type=jnp.float32) * scale).astype(jnp.bfloat16)
        return (attn, grad)
    attn_heads, grad_heads = lax.map(one_head, (split_heads(query, TEXT), split_heads(image_keys, IMG), split_heads(image_values, IMG), split_heads(upstream, TEXT), gate_tanh.reshape(HEADS, HEAD_DIM)))
    attn_rows = attn_heads.transpose(1, 0, 2).reshape(TEXT, CH)
    query_grad = grad_heads.transpose(1, 0, 2).reshape(TEXT, CH)
    attended = (gate_tanh[None, :] * attn_rows).astype(jnp.bfloat16)
    gate_grad = lax.optimization_barrier(jnp.sum(upstream * attn_rows, axis=0)) * (1.0 - gate_tanh * gate_tanh)

    def add_block(carry, pair):
        term = jnp.dot(pair[0].T, pair[1], preferred_element_type=jnp.float32)
        rounded = lax.optimization_barrier(term.astype(jnp.bfloat16)).astype(jnp.float32)
        return (carry + rounded, None)
    query_weight_grad = lax.scan(add_block, jnp.zeros((D, CH), jnp.float32), (normed_bf.reshape(N_IMG, TOK_DEV, D), query_grad.reshape(N_IMG, TOK_DEV, CH)))[0]
    normed_grad = jnp.dot(query_grad, w_query.T, preferred_element_type=jnp.float32)
    row_mean = lax.optimization_barrier(jnp.mean(normed_grad * normed, axis=1, keepdims=True))
    input_grad = (inverse_rms * (normed_grad - normed * row_mean)).astype(jnp.bfloat16)
    return (attended, input_grad, query_weight_grad, gate_grad)
```

```python
import functools
import math

import jax
import jax.numpy as jnp
from jax import lax
from jax.experimental import pallas as pl
from jax.experimental.pallas import tpu as pltpu
from jax.sharding import PartitionSpec as P

HEAD_DIM = 128
EPS = 1e-06
NEG = -1e30
SCALE = 1.0 / math.sqrt(HEAD_DIM)
BF16 = jnp.bfloat16
F32 = jnp.float32

STEP = {"x": 4, "y": 1}
AXES = (("x", "y"), ("y", "x"))
Z, X, Y, Z_LO, CORE = range(5)


def moved(i, axis, r):
    step = STEP[axis]
    at = (i // step) % 4
    return i + (((at + r) % 4) - at) * step


def pull(value, axis, r):
    return lax.ppermute(value, "img", [(i, moved(i, axis, -r)) for i in range(32)])


def pull_z(value):
    return lax.ppermute(value, "img", [(i, i ^ 16) for i in range(32)])


def pull_text(value, bit):
    return lax.ppermute(value, "text", [(i, i ^ bit) for i in range(4)])


def call(body, pos, inputs, outs, in_specs=None, out_specs=None, grid=(1,), scratch=(), after=(), us=0.6, vmem=24):
    def whole(shape):
        return pl.BlockSpec(shape, lambda i, pos: (0,) * len(shape))

    in_specs = list(in_specs) if in_specs else [None] * len(inputs)
    out_specs = list(out_specs) if out_specs else [None] * len(outs)
    in_specs = [s or whole(v.shape) for s, v in zip(in_specs, inputs)]
    out_specs = [s or whole(v.shape) for s, v in zip(out_specs, outs)]
    count = 1 + len(inputs)

    def kernel(*refs):
        body(*refs[:count], *refs[count + len(after):])

    return pl.pallas_call(
        kernel,
        grid_spec=pltpu.PrefetchScalarGridSpec(
            num_scalar_prefetch=1,
            grid=grid,
            in_specs=in_specs + [pl.BlockSpec(memory_space=pl.ANY)] * len(after),
            out_specs=out_specs,
            scratch_shapes=list(scratch),
        ),
        out_shape=list(outs),
        compiler_params=pltpu.CompilerParams(vmem_limit_bytes=vmem * 1024 * 1024),
        cost_estimate=pl.CostEstimate(flops=int(us * 1.0e9), bytes_accessed=int(us * 3.0e6), transcendentals=0),
    )(pos, *inputs, *after)


def like(shape, dtype=BF16):
    return jax.ShapeDtypeStruct(shape, dtype)


def lanes(start, size):
    return pl.ds(pl.multiple_of(start, 128), size)


def sum_parts(rows):
    rows = rows.astype(F32)
    return rows[0:1] + rows[1:2] + rows[2:3]


def three_parts(value):
    high = value.astype(BF16).astype(F32)
    middle = (value - high).astype(BF16).astype(F32)
    return [high, middle, value - high - middle]


def pack_body(pos, k_ref, v_ref, cot_ref, extra_ref, *outs):
    for s in range(2):
        at = pos[X + s]
        for r in range(4):
            column = s * 512 + ((at + 4 - r) % 4) * 128
            out = outs[s * 4 + r]
            out[0:64] = k_ref[:, lanes(column, 128)]
            out[64:128] = v_ref[:, lanes(column, 128)]
            out[128:144] = extra_ref[0:16]
            out[144:400] = cot_ref[:, lanes(column, 128)]
            out[400:416] = extra_ref[16:32]


def near_body(pos, *refs):
    for r in range(8):
        refs[8][r] = refs[r][...]


def merge_body(pos, near_ref, far_ref, *refs):
    count = len(refs) // 2
    refs[count][0:4] = near_ref[...]
    refs[count][4:8] = far_ref[...]
    for n in range(count):
        refs[count + 1 + n][...] = refs[n][...]


def copy_body(pos, *refs):
    count = len(refs) // 2
    for r in range(count):
        refs[count + r][...] = refs[r][...]


def stack_body(pos, *refs):
    for r in range(3):
        refs[3][r] = refs[r][...]


def norm_body(pos, x_ref, normed_ref, inverse_ref):
    x = x_ref[...].astype(F32)
    inverse = lax.rsqrt(jnp.mean(x * x, axis=1, keepdims=True) + EPS)
    inverse_ref[...] = jnp.broadcast_to(inverse, inverse_ref.shape)
    normed_ref[...] = (x * inverse).astype(BF16)


def query_body(pos, normed_ref, w0, w1, w2, w3, query_ref):
    step = pl.program_id(0)
    part = None
    for n, w_ref in enumerate((w0, w1, w2, w3)):
        term = jnp.dot(normed_ref[:, n * 256:(n + 1) * 256], w_ref[...], preferred_element_type=F32)
        part = term if part is None else part + term

    @pl.when(step == 0)
    def _():
        query_ref[...] = part

    @pl.when(step != 0)
    def _():
        query_ref[...] += part


def chunks_body(pos, query_ref, *outs):
    for s in range(2):
        for r in range(4):
            column = s * 512 + ((pos[X + s] + 4 - r) % 4) * 128
            outs[s * 4 + r][...] = query_ref[:, lanes(column, 128)].astype(BF16)


def attention_body(s, pos, *refs):
    queries, messages, quarters = refs[0:4], refs[4:8], refs[8:12]
    gate_ref, out_refs = refs[12], refs[13:17]
    q_s, cot_s, image_s, att_s, grad_ref, s_ref = refs[17:]
    pieces = [q.at[h * 4:h * 4 + 4] for q in quarters for h in range(2)]
    for r in range(4):
        q_s[r] = queries[r][...]
        cot_s[r] = messages[r][144:400]
        image_s[r] = messages[r][400:416]
    tanh = jnp.tanh(gate_ref[:, lanes(s * 512 + pos[X + s] * 128, 128)])

    def keys(i):
        return pieces[i][:, 0:64, :].reshape(256, HEAD_DIM)

    def values(i):
        return pieces[i][:, 64:128, :].reshape(256, HEAD_DIM)

    owners = []
    for i in range(8):
        for j in (0, 2):
            left = pieces[i][j, 128:144, :].astype(F32)
            right = pieces[i][j + 1, 128:144, :].astype(F32)
            owners.append(left[0:1] + right[1:2])

    def block(t, gate_sum):
        query = q_s[t]
        rows = image_s[t].astype(F32)
        image = jnp.concatenate(
            [jnp.transpose(jnp.broadcast_to(rows[h:h + 1], (128, 128))) for h in range(2)], 0
        )
        top = jnp.full((256, 128), NEG, F32)
        for i in range(8):
            sc = lax.dot_general(query, keys(i), (((1,), (1,)), ((), ())), preferred_element_type=F32)
            for h in range(2):
                part = jnp.where(image == owners[2 * i + h], sc[:, h * 128:(h + 1) * 128], NEG)
                s_ref[:, i * 256 + h * 128:i * 256 + (h + 1) * 128] = part
                top = jnp.maximum(top, part)
        peak = jnp.max(top, axis=1, keepdims=True)
        total = jnp.zeros((256, 128), F32)
        accum = jnp.zeros((256, HEAD_DIM), F32)
        for i in range(8):
            w = jnp.exp((s_ref[:, i * 256:(i + 1) * 256] - peak) * SCALE)
            s_ref[:, i * 256:(i + 1) * 256] = w
            total = total + (w[:, :128] + w[:, 128:])
            accum = accum + jnp.dot(w.astype(BF16), values(i), preferred_element_type=F32)
        inverse = 1.0 / jnp.sum(total, axis=1, keepdims=True)
        attn = accum * inverse
        upstream = cot_s[t].astype(F32)
        att_s[t] = (attn * tanh).astype(BF16)
        out_grad = upstream * tanh
        delta = jnp.sum(out_grad * attn, axis=1, keepdims=True)
        out_grad = out_grad.astype(BF16)
        grad = jnp.zeros((256, HEAD_DIM), F32)
        for i in range(8):
            dprob = lax.dot_general(out_grad, values(i), (((1,), (1,)), ((), ())), preferred_element_type=F32)
            dscore = ((s_ref[:, i * 256:(i + 1) * 256] * inverse) * (dprob - delta)).astype(BF16)
            grad = grad + jnp.dot(dscore, keys(i), preferred_element_type=F32)
        grad_ref[pl.ds(pl.multiple_of(t * 256, 256), 256)] = (grad * SCALE).astype(BF16)
        return gate_sum + jnp.sum(upstream * attn, axis=0, keepdims=True)

    gate_sum = lax.fori_loop(0, 4, block, jnp.zeros((1, HEAD_DIM), F32))
    grad_ref[1024:1040] = jnp.concatenate(three_parts(gate_sum) + [jnp.zeros((13, 128), F32)], 0).astype(BF16)
    for r in range(4):
        out_refs[r][0:1040] = grad_ref[...]
        out_refs[r][1040:1296] = att_s[(4 - r) % 4]


def product(half, b, parts):
    out = None
    for j in range(4):
        term = lax.dot_general(
            parts(half, j), b[j * 256:(j + 1) * 256], (((0,), (0,)), ((), ())), preferred_element_type=F32
        )
        out = term if out is None else out + term
    return out


def parts_of(refs):
    def part(half, j):
        if j == 0:
            return refs[half][...]
        return refs[5][j - 1] if half else refs[1 + j][...]

    return part


def first_body(s, pos, *refs):
    messages, part = refs[0:4], parts_of(refs[4:10])
    out_refs, keep_ref, gate_ref, b_ref = refs[10:13], refs[13], refs[14], refs[15]
    step = pl.program_id(0)

    @pl.when(step == 0)
    def _():
        for r in range(4):
            column = ((pos[X + s] + r) % 4) * 128
            for j in range(4):
                source = ((j - r) % 4) * 256
                b_ref[j * 256:(j + 1) * 256, lanes(column, 128)] = messages[r][source:source + 256]
            gate_ref[:, lanes(column, 128)] = sum_parts(messages[r][1024:1040])
        rows = jnp.concatenate(three_parts(gate_ref[...]) + [jnp.zeros((13, 512), F32)], 0).astype(BF16)
        for out_ref in out_refs:
            out_ref[512:528] = rows

    for half in range(2):
        rows = slice(half * 256, (half + 1) * 256)
        acc = product(half, b_ref, part)
        for n, out_ref in enumerate(out_refs):

            @pl.when(step == n)
            def _():
                out_ref[rows] = acc.astype(BF16)

        @pl.when(step == 3)
        def _():
            keep_ref[rows] = acc


def third_body(pos, *refs):
    keep_in, gate_ref, got = refs[0], refs[1], refs[2:5]
    send_ref, keep_ref, gate_out, total = refs[5:]
    for half in range(2):
        rows = slice(half * 256, (half + 1) * 256)
        total[half] = keep_in[rows] + (got[0][rows].astype(F32) + got[1][rows].astype(F32) + got[2][rows].astype(F32))
    keep = (pos[Z] + pos[CORE]) % 2
    send_ref[0:256] = total[1 - keep].astype(BF16)
    keep_ref[...] = total[keep]
    gate = gate_ref[...]
    for ref in got:
        gate = gate + sum_parts(ref[512:528])
    gate_out[...] = gate
    send_ref[256:272] = jnp.concatenate(three_parts(gate) + [jnp.zeros((13, 512), F32)], 0).astype(BF16)


def last_body(pos, *refs):
    gate_ref, out_ref, grad_ref = refs[0], refs[7], refs[8]
    tanh = jnp.tanh(gate_ref[...])
    for s in range(2):
        keep_ref, sum_ref, got_ref = refs[1 + 3 * s:4 + 3 * s]
        columns = slice(s * 512, (s + 1) * 512)
        out_ref[:, columns] = keep_ref[...] + got_ref[0:256].astype(F32)
        t = tanh[:, columns]
        grad_ref[:, columns] = (sum_ref[...] + sum_parts(got_ref[256:272])) * (1.0 - t * t)


def partial_grad(grad, w_refs):
    dims = (((1,), (1,)), ((), ()))
    return jnp.concatenate(
        [lax.dot_general(grad, w_ref[...], dims, preferred_element_type=F32) for w_ref in w_refs], 1
    )


def input_first_body(pos, *refs):
    messages = refs[0:8]
    query_ref, inverse_ref, x_ref, w0, w1, w2, w3, send_ref, share_ref, grad_ref = refs[8:]

    @pl.when(pl.program_id(0) == 0)
    def _():
        for s in range(2):
            for r in range(4):
                column = s * 512 + ((pos[X + s] + r) % 4) * 128
                source = ((4 - r) % 4) * 256
                grad_ref[:, lanes(column, 128)] = messages[s * 4 + r][source:source + 256]
        share = jnp.sum(grad_ref[...].astype(F32) * query_ref[...], axis=1, keepdims=True)
        share_ref[...] = jnp.broadcast_to(share * (1.0 / 8192.0), share_ref.shape)

    h = x_ref[...].astype(F32) * inverse_ref[:, :1]
    send_ref[...] = (partial_grad(grad_ref[...], (w0, w1, w2, w3)) - h * share_ref[:, :1]).astype(BF16)


def input_next_body(pos, grad_ref, share_ref, inverse_ref, x_ref, w0, w1, w2, w3, got_ref, out_ref):
    h = x_ref[...].astype(F32) * inverse_ref[:, :1]
    out = partial_grad(grad_ref[...], (w0, w1, w2, w3)) - h * share_ref[:, :1] + got_ref[...].astype(F32)
    out_ref[...] = out.astype(out_ref.dtype)


def input_last_body(pos, keep_ref, got_ref, inverse_ref, out_ref):
    out_ref[...] = ((keep_ref[...] + got_ref[...].astype(F32)) * inverse_ref[:, :1]).astype(BF16)


def home_body(pos, *refs):
    out_ref = refs[8]
    for s in range(2):
        for r in range(4):
            column = s * 512 + ((pos[X + s] + r) % 4) * 128
            out_ref[:, lanes(column, 128)] = refs[s * 4 + r][1040:1296]


def on_device(text_in, w_query, gate, image_keys, image_values, image_owner, text_image, cotangent):
    where, member = lax.axis_index("img"), lax.axis_index("text")
    pos = jnp.stack([where // 16, (where // 4) % 4, where % 4, member // 2, member % 2]).astype(jnp.int32)
    gate_row = gate.reshape(1, 1024)

    owner = image_owner.astype(BF16)
    empty = jnp.zeros((64,), BF16)
    pair = jnp.stack([jnp.concatenate([owner, empty]), jnp.concatenate([empty, owner])])
    extra = jnp.concatenate([jnp.tile(pair, (8, 1)), jnp.tile(text_image.astype(BF16).reshape(2, 128), (8, 1))], 0)
    packed = call(pack_body, pos, [image_keys, image_values, cotangent, extra], [like((416, 128))] * 8)
    first = []
    for s, (axis, other) in enumerate(AXES):
        mine = packed[s * 4:s * 4 + 4]
        first.append([mine[0]] + [pull(mine[r], axis, r) for r in (1, 2, 3)])
    rows = lambda width: pl.BlockSpec((32, width), lambda i, pos: (i, 0))
    normed, inverse = call(
        norm_body, pos, [text_in], [like((256, 8192)), like((256, 128), F32)],
        in_specs=[rows(8192)], out_specs=[rows(8192), rows(128)], grid=(8,), after=[packed[0]], us=2.6,
    )
    kv_rows = pl.BlockSpec((144, 128), lambda i, pos: (0, 0))
    near = call(near_body, pos, first[0] + first[1], [like((8, 144, 128))], in_specs=[kv_rows] * 8)[0]
    far = pull_z(near)

    def cut(s, backs, after):
        if s == 0:
            block = lambda r: pl.BlockSpec((256, 1024), lambda i, pos: (0, pos[CORE] * 4 + (pos[X] + 4 - r) % 4))
            out = pl.BlockSpec((256, 1024), lambda i, pos: (0, 0))
        else:
            block = lambda r: pl.BlockSpec(
                (256, 256), lambda i, pos: (0, pos[CORE] * 16 + i * 4 + (pos[Y] + 4 - r) % 4)
            )
            out = pl.BlockSpec((256, 256), lambda i, pos: (0, i))
        return call(
            copy_body, pos, [normed] * len(backs), [like((256, 1024))] * len(backs),
            in_specs=[block(r) for r in backs], out_specs=[out] * len(backs), grid=(1 + 3 * s,), after=after,
        )

    def stack(got, after=()):
        return call(stack_body, pos, got, [like((3, 256, 1024))], after=after)[0]

    quarter = lambda s: pl.BlockSpec((4, 144, 128), lambda i, pos: (s, 0, 0))

    def merge(s, others, after):
        mine, *rest = call(
            merge_body, pos, [near, far] + others, [like((8, 144, 128))] + [like((256, 128))] * len(others),
            in_specs=[quarter(s)] * 2 + [None] * len(others), after=after,
        )
        return [mine] + [pull(mine, AXES[s][1], r) for r in (1, 2, 3)], rest

    def attend(s, after):
        return call(
            functools.partial(attention_body, s), pos, queries[s] + first[s] + quarters[s] + [gate_row],
            [like((1296, 128))] * 4,
            scratch=[
                pltpu.VMEM((4, 256, 128), BF16),
                pltpu.VMEM((4, 256, 128), BF16),
                pltpu.VMEM((4, 16, 128), BF16),
                pltpu.VMEM((4, 256, 128), BF16),
                pltpu.VMEM((1040, 128), BF16),
                pltpu.VMEM((256, 2048), F32),
            ],
            after=after, us=8.5,
        )

    early = cut(0, (1, 3), [near])
    got_x = [pull(early[0], "x", 1), None, pull(early[1], "x", 3)]
    quarters = [merge(0, [], [early[0]])[0]]
    early = cut(0, (2,), [got_x[0], got_x[2]])
    got_x[1] = pull(early[0], "x", 2)
    query = call(
        query_body, pos, [normed] + [w_query] * 4,
        [like((256, 1024), F32)],
        in_specs=[
            pl.BlockSpec((256, 1024), lambda i, pos: (0, i)),
        ] + [pl.BlockSpec((256, 1024), lambda i, pos, n=n: (i * 4 + n, 0)) for n in range(4)],
        grid=(8,), after=[quarters[0][0], early[0]], us=11.0, vmem=48,
    )[0]
    chunks = call(chunks_body, pos, [query], [like((256, 128))] * 8, after=quarters[0][1:] + [got_x[1]])
    swapped = [pull_text(stack(got_x, [chunks[0]]), 1)]
    queries = [
        [chunks[s * 4]] + [pull(chunks[s * 4 + r], axis, r) for r in (1, 2, 3)] for s, (axis, other) in enumerate(AXES)
    ]
    quarters.append(merge(1, [], queries[0][1:] + queries[1][1:] + swapped)[0])
    late = cut(1, (1, 3, 2), [quarters[1][0]])
    results = [attend(0, late)]
    results.append(attend(1, [results[0][0]]))
    got_y = [pull(late[(0, 2, 1)[r - 1]], "y", r) for r in (1, 2, 3)]
    swapped.append(pull_text(stack(got_y, [results[1][0]]), 1))
    parts = [[normed, normed] + got + [swapped[s]] for s, got in enumerate((got_x, got_y))]

    def part_specs(s, order):
        axis = X + (1 - s)
        at = lambda i, pos: (pos[axis] + order(i)) % 4
        own = lambda i, pos: pos[X] * 4 + at(i, pos) if s == 0 else at(i, pos) * 4 + pos[Y]
        return (
            [
                pl.BlockSpec((256, 256), lambda i, pos: (0, pos[CORE] * 16 + own(i, pos))),
                pl.BlockSpec((256, 256), lambda i, pos: (0, (1 - pos[CORE]) * 16 + own(i, pos))),
            ]
            + [pl.BlockSpec((256, 256), lambda i, pos: (0, at(i, pos)))] * 3
            + [pl.BlockSpec((3, 256, 256), lambda i, pos: (0, 0, at(i, pos)))]
        )

    messages = []
    for s, (axis, other) in enumerate(AXES):
        mine = results[s]
        messages.append([mine[0]] + [pull(mine[r], axis, r) for r in (1, 2, 3)])

    def first_chunks(s, after):
        *sends, keep, gate_sum = call(
            functools.partial(first_body, s), pos, messages[s] + parts[s],
            [like((528, 512))] * 3 + [like((512, 512), F32), like((1, 512), F32)],
            in_specs=[None] * 4 + part_specs(s, lambda i: i + 1),
            scratch=[pltpu.VMEM((1024, 512), BF16)],
            grid=(4,), after=after, us=6.0,
        )
        got = [pull(v, AXES[s][1], -m) for v, m in zip(sends, (1, 2, 3))]
        return [keep, gate_sum] + got, sends[0]

    def third(s, values, after):
        message, keep, gate_total = call(
            third_body, pos, values, [like((272, 512)), like((256, 512), F32), like((1, 512), F32)],
            scratch=[pltpu.VMEM((2, 256, 512), F32)], after=after,
        )
        return [keep, gate_total, pull_z(message)]

    def column_specs(block):
        return [
            pl.BlockSpec((256, 1024), lambda i, pos: (0, block(i, pos))),
        ] + [pl.BlockSpec((256, 1024), lambda i, pos, n=n: (block(i, pos) * 4 + n, 0)) for n in range(4)]

    values0, done0 = first_chunks(0, [results[1][0]])
    send, share, grad_own = call(
        input_first_body, pos, messages[0] + messages[1] + [query, inverse, text_in] + [w_query] * 4,
        [like((256, 4096)), like((256, 128), F32), like((256, 1024))],
        in_specs=[None] * 10 + column_specs(lambda i, pos: (i // 2) * 4 + (1 - pos[CORE]) * 2 + i % 2),
        out_specs=[pl.BlockSpec((256, 1024), lambda i, pos: (0, i)), None, None],
        grid=(4,), after=[done0], us=8.0, vmem=48,
    )
    got_core = pull_text(send, 1)

    def input_next(z_of, dtype, after):
        return call(
            input_next_body, pos, [grad_own, share, inverse, text_in] + [w_query] * 4 + [got_core],
            [like((256, 2048), dtype)],
            in_specs=[None] * 3
            + column_specs(lambda i, pos: z_of(pos) * 4 + pos[CORE] * 2 + i)
            + [pl.BlockSpec((256, 1024), lambda i, pos: (0, z_of(pos) * 2 + i))],
            out_specs=[pl.BlockSpec((256, 1024), lambda i, pos: (0, i))],
            grid=(2,), after=after, us=4.0, vmem=48,
        )[0]

    values1, done1 = first_chunks(1, [send])
    send_z_lo = input_next(lambda pos: 1 - pos[Z_LO], BF16, [done1])
    closing = third(0, values0, [send_z_lo])
    got_z_lo = pull_text(send_z_lo, 2)
    keep_input = input_next(lambda pos: pos[Z_LO], F32, [closing[0]])
    attended = call(home_body, pos, messages[0] + messages[1], [like((256, 1024))], after=[keep_input])[0]
    closing += third(1, values1, [attended])
    query_weight_grad, gate_grad = call(
        last_body, pos, [gate_row] + closing, [like((256, 1024), F32), like((1, 1024), F32)], after=[closing[3]]
    )
    input_grad = call(input_last_body, pos, [keep_input, got_z_lo, inverse], [like((256, 2048))])[0]
    return (attended, input_grad, query_weight_grad, gate_grad.reshape(1024))


def solution(mesh):
    in_specs = (
        P("img", None),
        P(None, "text"),
        P("text"),
        P("img", "text"),
        P("img", "text"),
        P("img"),
        P("img"),
        P("img", "text"),
    )
    out_specs = (P("img", "text"), P("img", "text"), P("img", "text"), P("text"))
    return jax.shard_map(
        on_device, mesh=mesh, in_specs=in_specs, out_specs=out_specs, check_vma=False
    )
```

```python
import functools
import math

import jax
import jax.numpy as jnp
from jax import lax
from jax.experimental import pallas as pl
from jax.experimental.pallas import tpu as pltpu
from jax.sharding import PartitionSpec as P

HEAD_DIM = 128
EPS = 1e-06
NEG = -1e30
SCALE = 1.0 / math.sqrt(HEAD_DIM)
BF16 = jnp.bfloat16
F32 = jnp.float32

STEP = {"x": 4, "y": 1}
AXES = (("x", "y"), ("y", "x"))
Z, X, Y, Z_LO, CORE = range(5)


def moved(i, axis, r):
    step = STEP[axis]
    at = (i // step) % 4
    return i + (((at + r) % 4) - at) * step


def pull(value, axis, r):
    return lax.ppermute(value, "img", [(i, moved(i, axis, -r)) for i in range(32)])


def pull_z(value):
    return lax.ppermute(value, "img", [(i, i ^ 16) for i in range(32)])


def pull_text(value, bit):
    return lax.ppermute(value, "text", [(i, i ^ bit) for i in range(4)])


def call(body, pos, inputs, outs, in_specs=None, out_specs=None, grid=(1,), scratch=(), after=(), us=0.6, vmem=24):
    def whole(shape):
        return pl.BlockSpec(shape, lambda i, pos: (0,) * len(shape))

    in_specs = list(in_specs) if in_specs else [None] * len(inputs)
    out_specs = list(out_specs) if out_specs else [None] * len(outs)
    in_specs = [s or whole(v.shape) for s, v in zip(in_specs, inputs)]
    out_specs = [s or whole(v.shape) for s, v in zip(out_specs, outs)]
    count = 1 + len(inputs)

    def kernel(*refs):
        body(*refs[:count], *refs[count + len(after):])

    return pl.pallas_call(
        kernel,
        grid_spec=pltpu.PrefetchScalarGridSpec(
            num_scalar_prefetch=1,
            grid=grid,
            in_specs=in_specs + [pl.BlockSpec(memory_space=pl.ANY)] * len(after),
            out_specs=out_specs,
            scratch_shapes=list(scratch),
        ),
        out_shape=list(outs),
        compiler_params=pltpu.CompilerParams(vmem_limit_bytes=vmem * 1024 * 1024),
        cost_estimate=pl.CostEstimate(flops=int(us * 1.0e9), bytes_accessed=int(us * 3.0e6), transcendentals=0),
    )(pos, *inputs, *after)


def like(shape, dtype=BF16):
    return jax.ShapeDtypeStruct(shape, dtype)


def lanes(start, size):
    return pl.ds(pl.multiple_of(start, 128), size)


def sum_parts(rows):
    rows = rows.astype(F32)
    return rows[0:1] + rows[1:2] + rows[2:3]


def three_parts(value):
    high = value.astype(BF16).astype(F32)
    middle = (value - high).astype(BF16).astype(F32)
    return [high, middle, value - high - middle]


def pack_body(pos, k_ref, v_ref, cot_ref, extra_ref, *outs):
    for s in range(2):
        at = pos[X + s]
        for r in range(4):
            column = s * 512 + ((at + 4 - r) % 4) * 128
            out = outs[s * 4 + r]
            out[0:64] = k_ref[:, lanes(column, 128)]
            out[64:128] = v_ref[:, lanes(column, 128)]
            out[128:144] = extra_ref[0:16]
            out[144:400] = cot_ref[:, lanes(column, 128)]
            out[400:416] = extra_ref[16:32]


def near_body(pos, *refs):
    for r in range(8):
        refs[8][r] = refs[r][...]


def merge_body(pos, near_ref, far_ref, *refs):
    count = len(refs) // 2
    refs[count][0:4] = near_ref[...]
    refs[count][4:8] = far_ref[...]
    for n in range(count):
        refs[count + 1 + n][...] = refs[n][...]


def copy_body(pos, *refs):
    count = len(refs) // 2
    for r in range(count):
        refs[count + r][...] = refs[r][...]


def stack_body(pos, *refs):
    for r in range(3):
        refs[3][r] = refs[r][...]


def norm_body(pos, x_ref, normed_ref, inverse_ref):
    x = x_ref[...].astype(F32)
    inverse = lax.rsqrt(jnp.mean(x * x, axis=1, keepdims=True) + EPS)
    inverse_ref[...] = jnp.broadcast_to(inverse, inverse_ref.shape)
    normed_ref[...] = (x * inverse).astype(BF16)


def fetch(pairs, sem):
    copies = [pltpu.make_async_copy(source, target, sem.at[n]) for n, (source, target) in enumerate(pairs)]
    for copy in copies:
        copy.start()
    return copies


def query_body(pos, normed_ref, w_ref, query_ref, normed_buf, w_buf, sem):
    pairs = []
    for i in range(8):
        pairs.append((normed_ref.at[:, i * 1024:(i + 1) * 1024], normed_buf.at[i]))
        pairs.append((w_ref.at[i * 1024:(i + 1) * 1024], w_buf.at[i]))
    copies = fetch(pairs, sem)
    for i in range(8):
        copies[2 * i].wait()
        copies[2 * i + 1].wait()
        part = jnp.dot(normed_buf[i], w_buf[i], preferred_element_type=F32)
        query_ref[...] = part if i == 0 else query_ref[...] + part


def chunks_body(pos, query_ref, *outs):
    for s in range(2):
        for r in range(4):
            column = s * 512 + ((pos[X + s] + 4 - r) % 4) * 128
            outs[s * 4 + r][...] = query_ref[:, lanes(column, 128)].astype(BF16)


def attention_body(s, pos, *refs):
    queries, messages, quarters = refs[0:4], refs[4:8], refs[8:12]
    gate_ref, out_refs = refs[12], refs[13:17]
    q_s, cot_s, image_s, att_s, grad_ref, s_ref = refs[17:]
    pieces = [q.at[h * 4:h * 4 + 4] for q in quarters for h in range(2)]
    for r in range(4):
        q_s[r] = queries[r][...]
        cot_s[r] = messages[r][144:400]
        image_s[r] = messages[r][400:416]
    tanh = jnp.tanh(gate_ref[:, lanes(s * 512 + pos[X + s] * 128, 128)])

    def keys(i):
        return pieces[i][:, 0:64, :].reshape(256, HEAD_DIM)

    def values(i):
        return pieces[i][:, 64:128, :].reshape(256, HEAD_DIM)

    owners = []
    for i in range(8):
        for j in (0, 2):
            left = pieces[i][j, 128:144, :].astype(F32)
            right = pieces[i][j + 1, 128:144, :].astype(F32)
            owners.append(left[0:1] + right[1:2])

    def block(t, gate_sum):
        query = q_s[t]
        rows = image_s[t].astype(F32)
        image = jnp.concatenate(
            [jnp.transpose(jnp.broadcast_to(rows[h:h + 1], (128, 128))) for h in range(2)], 0
        )
        top = jnp.full((256, 128), NEG, F32)
        for i in range(8):
            sc = lax.dot_general(query, keys(i), (((1,), (1,)), ((), ())), preferred_element_type=F32)
            for h in range(2):
                part = jnp.where(image == owners[2 * i + h], sc[:, h * 128:(h + 1) * 128], NEG)
                s_ref[:, i * 256 + h * 128:i * 256 + (h + 1) * 128] = part
                top = jnp.maximum(top, part)
        peak = jnp.max(top, axis=1, keepdims=True)
        total = jnp.zeros((256, 128), F32)
        accum = jnp.zeros((256, HEAD_DIM), F32)
        for i in range(8):
            w = jnp.exp((s_ref[:, i * 256:(i + 1) * 256] - peak) * SCALE)
            s_ref[:, i * 256:(i + 1) * 256] = w
            total = total + (w[:, :128] + w[:, 128:])
            accum = accum + jnp.dot(w.astype(BF16), values(i), preferred_element_type=F32)
        inverse = 1.0 / jnp.sum(total, axis=1, keepdims=True)
        attn = accum * inverse
        upstream = cot_s[t].astype(F32)
        att_s[t] = (attn * tanh).astype(BF16)
        out_grad = upstream * tanh
        delta = jnp.sum(out_grad * attn, axis=1, keepdims=True)
        out_grad = out_grad.astype(BF16)
        grad = jnp.zeros((256, HEAD_DIM), F32)
        for i in range(8):
            dprob = lax.dot_general(out_grad, values(i), (((1,), (1,)), ((), ())), preferred_element_type=F32)
            dscore = ((s_ref[:, i * 256:(i + 1) * 256] * inverse) * (dprob - delta)).astype(BF16)
            grad = grad + jnp.dot(dscore, keys(i), preferred_element_type=F32)
        grad_ref[pl.ds(pl.multiple_of(t * 256, 256), 256)] = (grad * SCALE).astype(BF16)
        return gate_sum + jnp.sum(upstream * attn, axis=0, keepdims=True)

    gate_sum = lax.fori_loop(0, 4, block, jnp.zeros((1, HEAD_DIM), F32))
    grad_ref[1024:1040] = jnp.concatenate(three_parts(gate_sum) + [jnp.zeros((13, 128), F32)], 0).astype(BF16)
    for r in range(4):
        out_refs[r][0:1040] = grad_ref[...]
        out_refs[r][1040:1296] = att_s[(4 - r) % 4]


def product(half, b, parts):
    out = None
    for j in range(4):
        term = lax.dot_general(
            parts(half, j), b[j * 256:(j + 1) * 256], (((0,), (0,)), ((), ())), preferred_element_type=F32
        )
        out = term if out is None else out + term
    return out


def parts_of(refs):
    def part(half, j):
        if j == 0:
            return refs[half][...]
        return refs[5][j - 1] if half else refs[1 + j][...]

    return part


def first_body(s, pos, *refs):
    messages, part = refs[0:4], parts_of(refs[4:10])
    out_refs, keep_ref, gate_ref, b_ref = refs[10:13], refs[13], refs[14], refs[15]
    step = pl.program_id(0)

    @pl.when(step == 0)
    def _():
        for r in range(4):
            column = ((pos[X + s] + r) % 4) * 128
            for j in range(4):
                source = ((j - r) % 4) * 256
                b_ref[j * 256:(j + 1) * 256, lanes(column, 128)] = messages[r][source:source + 256]
            gate_ref[:, lanes(column, 128)] = sum_parts(messages[r][1024:1040])
        rows = jnp.concatenate(three_parts(gate_ref[...]) + [jnp.zeros((13, 512), F32)], 0).astype(BF16)
        for out_ref in out_refs:
            out_ref[512:528] = rows

    for half in range(2):
        rows = slice(half * 256, (half + 1) * 256)
        acc = product(half, b_ref, part)
        for n, out_ref in enumerate(out_refs):

            @pl.when(step == n)
            def _():
                out_ref[rows] = acc.astype(BF16)

        @pl.when(step == 3)
        def _():
            keep_ref[rows] = acc


def third_body(pos, *refs):
    keep_in, gate_ref, got = refs[0], refs[1], refs[2:5]
    send_ref, keep_ref, gate_out, total = refs[5:]
    for half in range(2):
        rows = slice(half * 256, (half + 1) * 256)
        total[half] = keep_in[rows] + (got[0][rows].astype(F32) + got[1][rows].astype(F32) + got[2][rows].astype(F32))
    keep = (pos[Z] + pos[CORE]) % 2
    send_ref[0:256] = total[1 - keep].astype(BF16)
    keep_ref[...] = total[keep]
    gate = gate_ref[...]
    for ref in got:
        gate = gate + sum_parts(ref[512:528])
    gate_out[...] = gate
    send_ref[256:272] = jnp.concatenate(three_parts(gate) + [jnp.zeros((13, 512), F32)], 0).astype(BF16)


def last_body(pos, *refs):
    gate_ref, out_ref, grad_ref = refs[0], refs[7], refs[8]
    tanh = jnp.tanh(gate_ref[...])
    for s in range(2):
        keep_ref, sum_ref, got_ref = refs[1 + 3 * s:4 + 3 * s]
        columns = slice(s * 512, (s + 1) * 512)
        out_ref[:, columns] = keep_ref[...] + got_ref[0:256].astype(F32)
        t = tanh[:, columns]
        grad_ref[:, columns] = (sum_ref[...] + sum_parts(got_ref[256:272])) * (1.0 - t * t)


def weight_rows(w_ref, w_buf, sem, blocks):
    return fetch(
        [(w_ref.at[pl.ds(pl.multiple_of(block * 1024, 1024), 1024)], w_buf.at[n]) for n, block in enumerate(blocks)], sem
    )


def partial_grad(grad, w, x, inverse, share):
    part = lax.dot_general(grad, w, (((1,), (1,)), ((), ())), preferred_element_type=F32)
    return part - x.astype(F32) * inverse * share


def input_first_body(pos, *refs):
    messages = refs[0:8]
    query_ref, inverse_ref, x0, x1, w_ref, send_ref, share_ref, grad_ref, w_buf, sem = refs[8:]
    copies = weight_rows(w_ref, w_buf, sem, [(i // 2) * 4 + (1 - pos[CORE]) * 2 + i % 2 for i in range(4)])
    for s in range(2):
        for r in range(4):
            column = s * 512 + ((pos[X + s] + r) % 4) * 128
            source = ((4 - r) % 4) * 256
            grad_ref[:, lanes(column, 128)] = messages[s * 4 + r][source:source + 256]
    grad = grad_ref[...]
    share = jnp.sum(grad.astype(F32) * query_ref[...], axis=1, keepdims=True) * (1.0 / 8192.0)
    share_ref[...] = jnp.broadcast_to(share, share_ref.shape)
    for i in range(4):
        x = (x0, x1)[i // 2][:, (i % 2) * 1024:(i % 2 + 1) * 1024]
        copies[i].wait()
        out = partial_grad(grad, w_buf[i], x, inverse_ref[:, :1], share)
        send_ref[:, i * 1024:(i + 1) * 1024] = out.astype(BF16)


def input_next_body(z_of, pos, grad_ref, share_ref, inverse_ref, x_ref, got_ref, w_ref, out_ref, w_buf, sem):
    copies = weight_rows(w_ref, w_buf, sem, [z_of(pos) * 4 + pos[CORE] * 2 + i for i in range(2)])
    for i in range(2):
        columns = slice(i * 1024, (i + 1) * 1024)
        copies[i].wait()
        out = partial_grad(grad_ref[...], w_buf[i], x_ref[:, columns], inverse_ref[:, :1], share_ref[:, :1])
        out_ref[:, columns] = (out + got_ref[:, columns].astype(F32)).astype(out_ref.dtype)


def input_last_body(pos, keep_ref, got_ref, inverse_ref, out_ref):
    out_ref[...] = ((keep_ref[...] + got_ref[...].astype(F32)) * inverse_ref[:, :1]).astype(BF16)


def home_body(pos, *refs):
    out_ref = refs[8]
    for s in range(2):
        for r in range(4):
            column = s * 512 + ((pos[X + s] + r) % 4) * 128
            out_ref[:, lanes(column, 128)] = refs[s * 4 + r][1040:1296]


def on_device(text_in, w_query, gate, image_keys, image_values, image_owner, text_image, cotangent):
    where, member = lax.axis_index("img"), lax.axis_index("text")
    pos = jnp.stack([where // 16, (where // 4) % 4, where % 4, member // 2, member % 2]).astype(jnp.int32)
    gate_row = gate.reshape(1, 1024)

    owner = image_owner.astype(BF16)
    empty = jnp.zeros((64,), BF16)
    pair = jnp.stack([jnp.concatenate([owner, empty]), jnp.concatenate([empty, owner])])
    extra = jnp.concatenate([jnp.tile(pair, (8, 1)), jnp.tile(text_image.astype(BF16).reshape(2, 128), (8, 1))], 0)
    packed = call(pack_body, pos, [image_keys, image_values, cotangent, extra], [like((416, 128))] * 8)
    first = []
    for s, (axis, other) in enumerate(AXES):
        mine = packed[s * 4:s * 4 + 4]
        first.append([mine[0]] + [pull(mine[r], axis, r) for r in (1, 2, 3)])
    rows = lambda width: pl.BlockSpec((32, width), lambda i, pos: (i, 0))
    normed, inverse = call(
        norm_body, pos, [text_in], [like((256, 8192)), like((256, 128), F32)],
        in_specs=[rows(8192)], out_specs=[rows(8192), rows(128)], grid=(8,), after=[packed[0]], us=2.6,
    )
    kv_rows = pl.BlockSpec((144, 128), lambda i, pos: (0, 0))
    near = call(near_body, pos, first[0] + first[1], [like((8, 144, 128))], in_specs=[kv_rows] * 8)[0]
    far = pull_z(near)

    def cut(s, backs, after):
        if s == 0:
            block = lambda r: pl.BlockSpec((256, 1024), lambda i, pos: (0, pos[CORE] * 4 + (pos[X] + 4 - r) % 4))
            out = pl.BlockSpec((256, 1024), lambda i, pos: (0, 0))
        else:
            block = lambda r: pl.BlockSpec(
                (256, 256), lambda i, pos: (0, pos[CORE] * 16 + i * 4 + (pos[Y] + 4 - r) % 4)
            )
            out = pl.BlockSpec((256, 256), lambda i, pos: (0, i))
        return call(
            copy_body, pos, [normed] * len(backs), [like((256, 1024))] * len(backs),
            in_specs=[block(r) for r in backs], out_specs=[out] * len(backs), grid=(1 + 3 * s,), after=after,
        )

    def stack(got, after=()):
        return call(stack_body, pos, got, [like((3, 256, 1024))], after=after)[0]

    quarter = lambda s: pl.BlockSpec((4, 144, 128), lambda i, pos: (s, 0, 0))

    def merge(s, others, after):
        mine, *rest = call(
            merge_body, pos, [near, far] + others, [like((8, 144, 128))] + [like((256, 128))] * len(others),
            in_specs=[quarter(s)] * 2 + [None] * len(others), after=after,
        )
        return [mine] + [pull(mine, AXES[s][1], r) for r in (1, 2, 3)], rest

    def attend(s, after):
        return call(
            functools.partial(attention_body, s), pos, queries[s] + first[s] + quarters[s] + [gate_row],
            [like((1296, 128))] * 4,
            scratch=[
                pltpu.VMEM((4, 256, 128), BF16),
                pltpu.VMEM((4, 256, 128), BF16),
                pltpu.VMEM((4, 16, 128), BF16),
                pltpu.VMEM((4, 256, 128), BF16),
                pltpu.VMEM((1040, 128), BF16),
                pltpu.VMEM((256, 2048), F32),
            ],
            after=after, us=8.5,
        )

    early = cut(0, (1, 3), [near])
    got_x = [pull(early[0], "x", 1), None, pull(early[1], "x", 3)]
    early = cut(1, (1, 3), early)
    got_y = [pull(early[0], "y", 1), None, pull(early[1], "y", 3)]
    quarters = [merge(0, [], [early[0]])[0]]
    early = cut(0, (2,), [got_x[0], got_x[2], got_y[0], got_y[2]])
    got_x[1] = pull(early[0], "x", 2)
    anywhere = pl.BlockSpec(memory_space=pl.ANY)
    query = call(
        query_body, pos, [normed, w_query], [like((256, 1024), F32)], in_specs=[anywhere] * 2,
        scratch=[
            pltpu.VMEM((8, 256, 1024), BF16),
            pltpu.VMEM((8, 1024, 1024), BF16),
            pltpu.SemaphoreType.DMA((16,)),
        ],
        after=[quarters[0][0], early[0]], us=11.0, vmem=44,
    )[0]
    chunks = call(chunks_body, pos, [query], [like((256, 128))] * 8, after=quarters[0][1:] + [got_x[1]])
    swapped = [pull_text(stack(got_x, [chunks[0]]), 1)]
    queries = [
        [chunks[s * 4]] + [pull(chunks[s * 4 + r], axis, r) for r in (1, 2, 3)] for s, (axis, other) in enumerate(AXES)
    ]
    quarters.append(merge(1, [], queries[0][1:] + queries[1][1:] + swapped)[0])
    late = cut(1, (2,), [quarters[1][0]])
    results = [attend(0, late)]
    results.append(attend(1, [results[0][0]]))
    got_y[1] = pull(late[0], "y", 2)
    swapped.append(pull_text(stack(got_y, [results[1][0]]), 1))
    parts = [[normed, normed] + got + [swapped[s]] for s, got in enumerate((got_x, got_y))]

    def part_specs(s, order):
        axis = X + (1 - s)
        at = lambda i, pos: (pos[axis] + order(i)) % 4
        own = lambda i, pos: pos[X] * 4 + at(i, pos) if s == 0 else at(i, pos) * 4 + pos[Y]
        return (
            [
                pl.BlockSpec((256, 256), lambda i, pos: (0, pos[CORE] * 16 + own(i, pos))),
                pl.BlockSpec((256, 256), lambda i, pos: (0, (1 - pos[CORE]) * 16 + own(i, pos))),
            ]
            + [pl.BlockSpec((256, 256), lambda i, pos: (0, at(i, pos)))] * 3
            + [pl.BlockSpec((3, 256, 256), lambda i, pos: (0, 0, at(i, pos)))]
        )

    messages = []
    for s, (axis, other) in enumerate(AXES):
        mine = results[s]
        messages.append([mine[0]] + [pull(mine[r], axis, r) for r in (1, 2, 3)])

    def first_chunks(s, after):
        *sends, keep, gate_sum = call(
            functools.partial(first_body, s), pos, messages[s] + parts[s],
            [like((528, 512))] * 3 + [like((512, 512), F32), like((1, 512), F32)],
            in_specs=[None] * 4 + part_specs(s, lambda i: i + 1),
            scratch=[pltpu.VMEM((1024, 512), BF16)],
            grid=(4,), after=after, us=6.0 if s == 0 else 0.1,
        )
        got = [pull(v, AXES[s][1], -m) for v, m in zip(sends, (1, 2, 3))]
        return [keep, gate_sum] + got, sends[0]

    def third(s, values, after):
        message, keep, gate_total = call(
            third_body, pos, values, [like((272, 512)), like((256, 512), F32), like((1, 512), F32)],
            scratch=[pltpu.VMEM((2, 256, 512), F32)], after=after, us=0.1,
        )
        return [keep, gate_total, pull_z(message)]

    values0, done0 = first_chunks(0, [results[1][0]])
    columns = lambda block: pl.BlockSpec((256, 2048), lambda i, pos: (0, block(pos)))
    send, share, grad_own = call(
        input_first_body, pos, messages[0] + messages[1] + [query, inverse, text_in, text_in, w_query],
        [like((256, 4096)), like((256, 128), F32), like((256, 1024))],
        in_specs=[None] * 10
        + [columns(lambda pos: 1 - pos[CORE]), columns(lambda pos: 3 - pos[CORE]), anywhere],
        scratch=[pltpu.VMEM((4, 1024, 1024), BF16), pltpu.SemaphoreType.DMA((4,))],
        after=[done0], us=8.0, vmem=40,
    )
    got_core = pull_text(send, 1)

    def input_next(z_of, dtype, after):
        return call(
            functools.partial(input_next_body, z_of), pos, [grad_own, share, inverse, text_in, got_core, w_query],
            [like((256, 2048), dtype)],
            in_specs=[None] * 3 + [columns(lambda pos: z_of(pos) * 2 + pos[CORE]), columns(z_of), anywhere],
            scratch=[pltpu.VMEM((2, 1024, 1024), BF16), pltpu.SemaphoreType.DMA((2,))],
            after=after, us=0.1, vmem=40,
        )[0]

    values1, done1 = first_chunks(1, [send])
    send_z_lo = input_next(lambda pos: 1 - pos[Z_LO], BF16, [done1])
    closing = third(0, values0, [send_z_lo])
    got_z_lo = pull_text(send_z_lo, 2)
    keep_input = input_next(lambda pos: pos[Z_LO], F32, [closing[0]])
    attended = call(home_body, pos, messages[0] + messages[1], [like((256, 1024))], after=[keep_input], us=0.1)[0]
    closing += third(1, values1, [attended])
    input_grad = call(input_last_body, pos, [keep_input, got_z_lo, inverse], [like((256, 2048))])[0]
    query_weight_grad, gate_grad = call(
        last_body, pos, [gate_row] + closing, [like((256, 1024), F32), like((1, 1024), F32)], after=[closing[3], input_grad]
    )
    return (attended, input_grad, query_weight_grad, gate_grad.reshape(1024))


def solution(mesh):
    in_specs = (
        P("img", None),
        P(None, "text"),
        P("text"),
        P("img", "text"),
        P("img", "text"),
        P("img"),
        P("img"),
        P("img", "text"),
    )
    out_specs = (P("img", "text"), P("img", "text"), P("img", "text"), P("text"))
    return jax.shard_map(
        on_device, mesh=mesh, in_specs=in_specs, out_specs=out_specs, check_vma=False
    )
```
